32 devices in a mesh: dp: 16 (over z, y, x), tensor: 2 (over core).
Axes of the slice: x: 2, y: 2, z: 4, core: 2. Of those that a mesh axis runs over, the one named last changes fastest.
Arguments:
- tokens: bfloat16 [32768, 768], P('dp'), may hold values from -6 to 6
- query_weight: bfloat16 [768, 768], P('dp', 'tensor'), may hold values from -0.21875 to 0.21875
- key_weight: bfloat16 [768, 768], P('dp', 'tensor'), may hold values from -0.21875 to 0.21875
- value_weight: bfloat16 [768, 768], P('dp', 'tensor'), may hold values from -0.21875 to 0.21875
- output_weight: bfloat16 [768, 768], P('dp', 'tensor'), may hold values from -1.75 to 1.75
- up_weight: bfloat16 [768, 3072], P('dp', 'tensor'), may hold values from -0.21875 to 0.21875
- down_weight: bfloat16 [768, 3072], P('dp', 'tensor'), may hold values from -0.109375 to 0.109375
- query_bias: float32 [768], P('tensor'), may hold values from -3 to 3
- value_bias: float32 [768], P('tensor'), may hold values from -3 to 3
- output_bias: float32 [768], replicated, may hold values from -0.6 to 0.6
- first_gain: float32 [768], replicated, may hold values from 0.5 to 1.5
- first_shift: float32 [768], replicated, may hold values from -0.6 to 0.6
- up_bias: float32 [3072], P('tensor'), may hold values from -3 to 3
- down_bias: float32 [768], replicated, may hold values from -0.6 to 0.6
- second_gain: float32 [768], replicated, may hold values from 0.5 to 1.5
- second_shift: float32 [768], replicated, may hold values from -0.6 to 0.6
- group_sizes: int32 [8], replicated, may hold values from 1 to 128, 256 in all
- sentence_order: int32 [512], replicated, may hold values from 0 to 511, each once
Outputs:
- pair_loss: float32 [], replicated
- grad_tokens: float32 [32768, 768], P('dp')
- grad_query_weight: float32 [768, 768], P('dp', 'tensor')
- grad_key_weight: float32 [768, 768], P('dp', 'tensor')
- grad_value_weight: float32 [768, 768], P('dp', 'tensor')
- grad_output_weight: float32 [768, 768], P('dp', 'tensor')
- grad_up_weight: float32 [768, 3072], P('dp', 'tensor')
- grad_down_weight: float32 [768, 3072], P('dp', 'tensor')
- grad_query_bias: float32 [768], P('tensor')
- grad_value_bias: float32 [768], P('tensor')
- grad_output_bias: float32 [768], replicated
- grad_first_gain: float32 [768], replicated
- grad_first_shift: float32 [768], replicated
- grad_up_bias: float32 [3072], P('tensor')
- grad_down_bias: float32 [768], replicated
- grad_second_gain: float32 [768], replicated
- grad_second_shift: float32 [768], replicated
The draws below stay inside these ranges and needn't reach their ends.
Inputs may be any that keep to these rules, and one draw needn't show every extreme that they name: Group g holds the pairs from group_sizes[0] + ... + group_sizes[g - 1] onward; the sizes add up to 256 and the largest is 128. A permutation of the sentences: pair p has source sentence_order[p] and target sentence_order[256 + p].
All inputs are finite; a program needn't handle non-finite values.
Results may differ from the reference program's by a relative error of at most 0.02.
Values may be sent and summed in bfloat16 or wider, within the bound.
No kernel may reach another device: no remote copies, remote signals or barrier semaphores. Data moves between devices by JAX's collectives and lax.ppermute only.
A program may use at most 192 MiB of HBM per device.

```python
import math
import jax
import jax.numpy as jnp
import numpy as np
from jax import lax

D = 768
HEADS = 12
HD = 64
FF = 3072
SEQ = 64
GROUPS = 8
SENTENCES = 512
PAIRS = 256
TOKENS = 32768
N_TENSOR = 2


def steps_of(stream_key, dims, cuts, least, top_value):
    loudness = 1.0
    for dim, parts in cuts:
        draws = jax.random.uniform(jax.random.fold_in(jax.random.fold_in(stream_key, 6), dim), (parts,), jnp.float32, least / len(cuts), top_value / len(cuts))
        loudness = loudness * jnp.repeat(jnp.exp(draws), dims[dim] // parts).reshape((-1,) + (1,) * (len(dims) - 1 - dim))
    return loudness


def split_up(count, total, reach, skew):
    portions = [(1 << 20) // math.isqrt(rank ** skew) + 1 for rank in range(2, count + 1)]
    rest, holding = total - reach - (count - 1), [1] * (count - 1)
    while rest > 0:
        movable = [i for i in range(count - 1) if holding[i] < reach]
        whole, remaining = sum([portions[i] for i in movable]), rest
        for i in movable:
            addition = min(reach - holding[i], max(1, remaining * portions[i] // whole), rest)
            holding[i] = holding[i] + addition
            rest = rest - addition
    return np.array([reach] + holding)


def uneven_parts(rng, number_of, total, most, skew):
    if number_of == 2:
        one = jax.random.randint(rng, (), max(1, total - most), min(most, total - 1) + 1)
        return jnp.stack([one, total - one])
    sizes = jnp.asarray(split_up(number_of, total, most, skew), jnp.int32)
    couples = (number_of - 1) // 2
    giver, receiver = sizes[1:1 + 2 * couples:2], sizes[2:2 + 2 * couples:2]
    room = jnp.minimum(giver - 1, most - receiver)
    shifted = jax.random.randint(jax.random.fold_in(rng, 1), (couples,), 0, 1 << 20) % (room + 1)
    sizes = sizes.at[1:1 + 2 * couples:2].set(giver - shifted).at[2:2 + 2 * couples:2].set(receiver + shifted)
    return sizes[jax.random.permutation(jax.random.fold_in(rng, 2), number_of)]


def bell_draw(rng, extent, scale, most, split=(), kind=jnp.bfloat16):
    loudness = steps_of(rng, extent, split, -0.22, 0.18) if split else 1.0
    array = jax.random.normal(rng, extent, jnp.float32) * scale * loudness
    return jnp.minimum(jnp.maximum(array, -most), most).astype(kind)


def setup_inputs(seed: int = 0) -> dict:
    key_of = jax.random.split(jax.random.key(seed), 19)
    return {
        "tokens": bell_draw(key_of[0], (TOKENS, D), 1.0, 6.0, ((0, 16),)),
        "query_weight": bell_draw(key_of[1], (D, D), D ** -0.5, 0.21875, ((0, 16), (1, 2))),
        "key_weight": bell_draw(key_of[2], (D, D), D ** -0.5, 0.21875, ((0, 16), (1, 2))),
        "value_weight": bell_draw(key_of[3], (D, D), D ** -0.5, 0.21875, ((0, 16), (1, 2))),
        "output_weight": bell_draw(key_of[4], (D, D), (D // SEQ) ** -0.5, 1.75, ((0, 16), (1, 2))),
        "up_weight": bell_draw(key_of[5], (D, FF), D ** -0.5, 0.21875, ((0, 16), (1, 2))),
        "down_weight": bell_draw(key_of[6], (D, FF), FF ** -0.5, 0.109375, ((0, 16), (1, 2))),
        "query_bias": bell_draw(key_of[7], (D,), 0.5, 3.0, ((0, 2),), jnp.float32),
        "value_bias": bell_draw(key_of[8], (D,), 0.5, 3.0, ((0, 2),), jnp.float32),
        "output_bias": bell_draw(key_of[9], (D,), 0.1, 0.6, (), jnp.float32),
        "first_gain": jnp.clip(1.0 + 0.1 * jax.random.normal(key_of[10], (D,), jnp.float32), 0.5, 1.5),
        "first_shift": bell_draw(key_of[11], (D,), 0.1, 0.6, (), jnp.float32),
        "up_bias": bell_draw(key_of[12], (FF,), 0.5, 3.0, ((0, 2),), jnp.float32),
        "down_bias": bell_draw(key_of[13], (D,), 0.1, 0.6, (), jnp.float32),
        "second_gain": jnp.clip(1.0 + 0.1 * jax.random.normal(key_of[14], (D,), jnp.float32), 0.5, 1.5),
        "second_shift": bell_draw(key_of[15], (D,), 0.1, 0.6, (), jnp.float32),
        "group_sizes": uneven_parts(key_of[16], GROUPS, PAIRS, PAIRS // 2, 2).astype(jnp.int32),
        "sentence_order": jax.random.permutation(key_of[17], SENTENCES).astype(jnp.int32),
    }


@jax.custom_vjp
def low(v):
    return lax.optimization_barrier(v.astype(jnp.bfloat16)).astype(jnp.float32)

@jax.custom_vjp
def low_back(v):
    return v

def low_keep(v):
    return (low(v), None)

def low_pass(kept, grad):
    return (grad,)

def back_keep(v):
    return (v, None)

def back_low(kept, grad):
    return (low(grad),)
low.defvjp(low_keep, low_pass)
low_back.defvjp(back_keep, back_low)
score_scale = 40.0
margin = 0.3
loss_scale = 65536.0
norm_eps = 1e-06
masked_score = -30000.0
precise = lax.Precision.HIGHEST

def dense(left, right):
    return jnp.dot(left, right, precision=precise)

def dense_last(left, right):
    return lax.dot_general(left, right, (((1,), (1,)), ((), ())), precision=precise)

def norm_rows(values, gain_vec, shift_vec):
    centre = lax.optimization_barrier(jnp.mean(values, axis=-1, keepdims=True))
    spread = lax.optimization_barrier(jnp.mean(jnp.square(values - centre), axis=-1, keepdims=True))
    return (values - centre) * lax.rsqrt(spread + norm_eps) * gain_vec + shift_vec

def soft_rows(values):
    raised = jnp.exp(values - lax.optimization_barrier(jnp.max(values, axis=-1, keepdims=True)))
    return raised / lax.optimization_barrier(jnp.sum(raised, axis=-1, keepdims=True))

def log_total(values, axis_num):
    peak = lax.optimization_barrier(jnp.max(values, axis=axis_num, keepdims=True))
    return jnp.squeeze(peak, axis_num) + jnp.log(lax.optimization_barrier(jnp.sum(jnp.exp(values - peak), axis=axis_num)))

def layer_block(inputs, params):
    query_weight, key_weight, value_weight, output_weight, up_weight, down_weight, query_bias, value_bias, output_bias, first_gain, first_shift, up_bias, down_bias, second_gain, second_shift = params
    row_count = inputs.shape[0]
    sentences = row_count // SEQ
    head_cols = D // N_TENSOR
    hidden_cols = FF // N_TENSOR
    head_shape = (sentences, SEQ, HEADS // N_TENSOR, HD)
    attn_scale = HD ** (-0.5)
    attention_total = jnp.zeros((row_count, D), inputs.dtype)
    for portion in range(N_TENSOR):
        columns = slice(portion * head_cols, (portion + 1) * head_cols)
        inputs_part = low_back(inputs)
        queries = low_back(low(dense(inputs_part, query_weight[:, columns]) + query_bias[columns]))
        key_rows = low_back(low(dense(inputs_part, key_weight[:, columns])))
        values = low_back(low(dense(inputs_part, value_weight[:, columns]) + value_bias[columns]))
        scores = low_back(jnp.einsum('sqhd,skhd->shqk', queries.reshape(head_shape), key_rows.reshape(head_shape), precision=precise) * attn_scale)
        attn_probs = low(soft_rows(scores))
        context = jnp.einsum('shqk,skhd->sqhd', attn_probs, values.reshape(head_shape), precision=precise)
        context = low_back(low(context.reshape(row_count, head_cols)))
        attention_total = attention_total + low(dense_last(context, output_weight[:, columns]))
    residual = inputs + low_back(attention_total) + output_bias
    hidden_first = norm_rows(residual, first_gain, first_shift)
    hidden_low = low(hidden_first)
    ffn_total = jnp.zeros((row_count, D), inputs.dtype)
    for portion in range(N_TENSOR):
        columns = slice(portion * hidden_cols, (portion + 1) * hidden_cols)
        hidden_part = low_back(hidden_low)
        pre_act = low_back(dense(hidden_part, up_weight[:, columns]) + up_bias[columns])
        activation = low(jax.nn.gelu(pre_act, approximate=False))
        ffn_total = ffn_total + low(dense_last(activation, down_weight[:, columns]))
    second = hidden_first + low_back(ffn_total) + down_bias
    output = norm_rows(second, second_gain, second_shift)
    return lax.optimization_barrier(jnp.mean(output.reshape(sentences, SEQ, D), axis=1))

def margin_loss(pooled, group_sizes, sentence_order):
    inverse = lax.rsqrt(lax.optimization_barrier(jnp.sum(pooled * pooled, axis=-1, keepdims=True)) + norm_eps)
    units = low(pooled * inverse)
    sources = jnp.take(units, sentence_order[:PAIRS], axis=0)
    targets = jnp.take(units, sentence_order[PAIRS:], axis=0)
    group_ends = jnp.cumsum(group_sizes)
    pair_ids = jnp.arange(PAIRS, dtype=jnp.int32)
    group_of = lax.optimization_barrier(jnp.sum((pair_ids[:, None] >= group_ends[None, :]).astype(jnp.int32), axis=1)).astype(jnp.int32)
    block_rows = min(512, PAIRS)

    def one_block(offset):
        row_ids = offset + jnp.arange(block_rows, dtype=jnp.int32)
        row_units = lax.dynamic_slice_in_dim(sources, offset, block_rows, 0)
        row_groups = lax.dynamic_slice_in_dim(group_of, offset, block_rows, 0)
        is_same = row_ids[:, None] == pair_ids[None, :]
        scores = low_back(score_scale * dense_last(row_units, targets))
        scores = scores - score_scale * margin * is_same.astype(scores.dtype)
        scores = jnp.where(row_groups[:, None] == group_of[None, :], scores, masked_score)
        diagonal = lax.optimization_barrier(jnp.sum(jnp.where(is_same, scores, 0.0), axis=1))
        return (log_total(scores, 1), log_total(scores, 0), diagonal)
    offsets = jnp.arange(PAIRS // block_rows, dtype=jnp.int32) * block_rows
    row_lse, col_parts, diagonal = lax.map(jax.checkpoint(one_block), offsets)
    col_lse = log_total(col_parts, 0)
    return jnp.mean(row_lse.reshape(PAIRS) + col_lse - 2.0 * diagonal.reshape(PAIRS))

def reference(tokens, query_weight, key_weight, value_weight, output_weight, up_weight, down_weight, query_bias, value_bias, output_bias, first_gain, first_shift, up_bias, down_bias, second_gain, second_shift, group_sizes, sentence_order):
    inputs = tokens.astype(jnp.float32)
    params = tuple((argument.astype(jnp.float32) for argument in (query_weight, key_weight, value_weight, output_weight, up_weight, down_weight, query_bias, value_bias, output_bias, first_gain, first_shift, up_bias, down_bias, second_gain, second_shift)))
    block_sent = min(64, SENTENCES)

    def objective(layer_in, layer_params):
        shaped = layer_in.reshape(SENTENCES // block_sent, block_sent * SEQ, D)
        pooled = lax.map(jax.checkpoint(lambda group_rows: layer_block(group_rows, layer_params)), shaped)
        return margin_loss(pooled.reshape(SENTENCES, D), group_sizes, sentence_order)
    loss_value, backward = jax.vjp(objective, inputs, params)
    grad_inputs, grads = backward(jnp.asarray(loss_scale, loss_value.dtype))
    return (loss_value, grad_inputs, grads[0], grads[1], grads[2], grads[3], grads[4], grads[5], grads[6], grads[7], grads[8], grads[9], grads[10], grads[11], grads[12], grads[13], grads[14])
```

```python
import functools

import jax
import jax.numpy as jnp
from jax import lax
from jax.experimental import pallas as pl
from jax.experimental.pallas import tpu as pltpu
from jax.sharding import PartitionSpec as P

D = 768
HD = 64
SEQ = 64

score_scale = 40.0
margin = 0.3
loss_scale = 65536.0
norm_eps = 1e-06
masked_score = -30000.0

bf16 = jnp.bfloat16
f32 = jnp.float32

ALONG_Z = (4, 8, 12)
IN_PLANE = (1, 2, 3)


def contract(left, right, left_dim, right_dim):
    return lax.dot_general(
        left, right, (((left_dim,), (right_dim,)), ((), ())), preferred_element_type=f32
    )


def product(left, right):
    return contract(left, right, 1, 0)


def contract_last(left, right):
    return contract(left, right, 1, 1)


def contract_first(left, right):
    return contract(left, right, 0, 0)


def swap_cores(array):
    return lax.ppermute(array, "tensor", [(0, 1), (1, 0)])


def swap_chips(array, mask):
    count = lax.axis_size("dp")
    return lax.ppermute(array, "dp", [(i, i ^ mask) for i in range(count)])


def gather_pieces(shard, first, second):
    near = jnp.concatenate([shard] + [swap_chips(shard, mask) for mask in first], axis=0)
    return [near] + [swap_chips(near, mask) for mask in second]


def reduce_pieces(slabs, first, second):
    total = slabs[0].astype(f32)
    for slab, mask in zip(slabs[1:], first):
        total = total + swap_chips(slab, mask).astype(f32)
    rows = total.shape[0] // 4
    total = total.astype(bf16)
    own = total[:rows].astype(f32)
    for i, mask in enumerate(second):
        part = lax.slice_in_dim(total, (i + 1) * rows, (i + 2) * rows, axis=0)
        own = own + swap_chips(part, mask).astype(f32)
    return own


def sum_small(array):
    for group in (ALONG_Z, IN_PLANE):
        a, b, c = [swap_chips(array, mask) for mask in group]
        array = (array + a) + (b + c)
    return array


def ordered(first, second):
    return [(j, i, a ^ b) for j, b in enumerate((0, *second)) for i, a in enumerate((0, *first))]


def place_kernel(order, rows, me_ref, *refs):
    pieces, full, sem = refs[:4], refs[4], refs[5]
    me = me_ref[0]
    copies = []
    for k, (j, i, mask) in enumerate(order):
        to = pl.multiple_of((me ^ mask) * rows, 16)
        copies.append(
            pltpu.make_async_copy(pieces[j].at[pl.ds(i * rows, rows)], full.at[pl.ds(to, rows)], sem.at[k])
        )
    for copy in copies:
        copy.start()
    for copy in copies:
        copy.wait()


def place_rows(pieces, first, second, me):
    rows = pieces[0].shape[0] // 4
    width = pieces[0].shape[1]
    return pl.pallas_call(
        functools.partial(place_kernel, ordered(first, second), rows),
        out_shape=jax.ShapeDtypeStruct((rows * 16, width), pieces[0].dtype),
        in_specs=[pl.BlockSpec(memory_space=pltpu.SMEM)] + [pl.BlockSpec(memory_space=pl.ANY)] * 4,
        out_specs=pl.BlockSpec(memory_space=pl.ANY),
        scratch_shapes=[pltpu.SemaphoreType.DMA((16,))],
        name="place_rows",
    )(me, *pieces)


def split_kernel(order, rows, me_ref, full, *refs):
    pieces, sem = refs[:4], refs[4]
    me = me_ref[0]
    copies = []
    for k, (j, i, mask) in enumerate(order):
        at = pl.multiple_of((me ^ mask) * rows, 16)
        copies.append(
            pltpu.make_async_copy(full.at[pl.ds(at, rows)], pieces[j].at[pl.ds(i * rows, rows)], sem.at[k])
        )
    for copy in copies:
        copy.start()
    for copy in copies:
        copy.wait()


def split_rows(full, first, second, me):
    rows = full.shape[0] // 16
    width = full.shape[1]
    return pl.pallas_call(
        functools.partial(split_kernel, ordered(second, first), rows),
        out_shape=[jax.ShapeDtypeStruct((rows * 4, width), full.dtype)] * 4,
        in_specs=[pl.BlockSpec(memory_space=pltpu.SMEM), pl.BlockSpec(memory_space=pl.ANY)],
        out_specs=[pl.BlockSpec(memory_space=pl.ANY)] * 4,
        scratch_shapes=[pltpu.SemaphoreType.DMA((16,))],
        name="split_rows",
    )(me, full)


def exact_gelu(values):
    return jax.nn.gelu(values, approximate=False)


def norm_forward(values, gain_vec, shift_vec):
    centre = jnp.mean(values, axis=-1, keepdims=True)
    spread = jnp.mean(jnp.square(values - centre), axis=-1, keepdims=True)
    inv_scale = lax.rsqrt(spread + norm_eps)
    normed = (values - centre) * inv_scale
    return (normed * gain_vec + shift_vec, normed, inv_scale)


def norm_backward(upstream, normed, inv_scale, gain_vec):
    scaled = upstream * gain_vec
    first_mean = jnp.mean(scaled, axis=-1, keepdims=True)
    second_mean = jnp.mean(scaled * normed, axis=-1, keepdims=True)
    grad_in = inv_scale * (scaled - first_mean - normed * second_mean)
    return (grad_in, jnp.sum(upstream * normed, axis=0), jnp.sum(upstream, axis=0))


def pair_objective(unit_low, pooled, group_sizes, sentence_order, device):
    total_sent = unit_low.shape[0]
    pair_count = total_sent // 2
    own_count = pooled.shape[0]
    sources = jnp.take(unit_low, sentence_order[:pair_count], axis=0)
    targets = jnp.take(unit_low, sentence_order[pair_count:], axis=0)
    group_ends = jnp.cumsum(group_sizes)
    pair_ids = jnp.arange(pair_count, dtype=jnp.int32)
    group_of = jnp.sum((pair_ids[:, None] >= group_ends[None, :]).astype(jnp.int32), axis=1)
    block_rows = min(512, pair_count)

    def scan_step(carried, offset):
        col_peak, col_total = carried
        row_ids = offset + jnp.arange(block_rows, dtype=jnp.int32)
        row_units = lax.dynamic_slice_in_dim(sources, offset, block_rows, 0)
        row_groups = lax.dynamic_slice_in_dim(group_of, offset, block_rows, 0)
        is_same = row_ids[:, None] == pair_ids[None, :]
        scores = score_scale * contract_last(row_units, targets)
        scores = scores - score_scale * margin * is_same.astype(jnp.float32)
        scores = jnp.where(row_groups[:, None] == group_of[None, :], scores, masked_score)
        row_peak = jnp.max(scores, axis=1, keepdims=True)
        row_lse = row_peak[:, 0] + jnp.log(jnp.sum(jnp.exp(scores - row_peak), axis=1))
        diagonal = jnp.sum(jnp.where(is_same, scores, 0.0), axis=1)
        new_peak = jnp.maximum(col_peak, jnp.max(scores, axis=0))
        new_total = col_total * jnp.exp(col_peak - new_peak) + jnp.sum(
            jnp.exp(scores - new_peak[None, :]), axis=0
        )
        return ((new_peak, new_total), (row_lse, diagonal))

    offsets = jnp.arange(pair_count // block_rows, dtype=jnp.int32) * block_rows
    start_state = (
        jnp.full((pair_count,), -1e30, jnp.float32),
        jnp.zeros((pair_count,), jnp.float32),
    )
    (col_peak, col_total), (row_lse, diagonal) = lax.scan(scan_step, start_state, offsets)
    col_lse = col_peak + jnp.log(col_total)
    row_lse = row_lse.reshape(pair_count)
    diagonal = diagonal.reshape(pair_count)
    loss_value = jnp.mean(row_lse + col_lse - 2.0 * diagonal)
    own_ids = device * own_count + jnp.arange(own_count, dtype=jnp.int32)
    matches = sentence_order[None, :] == own_ids[:, None]
    position = jnp.sum(
        jnp.where(matches, jnp.arange(total_sent, dtype=jnp.int32)[None, :], 0), axis=1
    )
    is_source = position < pair_count
    own_pair = jnp.where(is_source, position, position - pair_count)
    own_inverse = lax.rsqrt(jnp.sum(pooled * pooled, axis=-1, keepdims=True) + norm_eps)
    own_unit = pooled * own_inverse
    own_low = own_unit.astype(jnp.bfloat16)
    source_rows = is_source[:, None]
    pair_match = own_pair[:, None] == pair_ids[None, :]
    toward_targets = score_scale * contract_last(own_low, targets)
    toward_sources = score_scale * contract_last(own_low, sources)
    own_scores = jnp.where(source_rows, toward_targets, toward_sources)
    own_scores = own_scores - score_scale * margin * pair_match.astype(jnp.float32)
    own_group = jnp.sum(jnp.where(pair_match, group_of[None, :], 0), axis=1)
    own_scores = jnp.where(own_group[:, None] == group_of[None, :], own_scores, masked_score)
    own_lse = jnp.sum(
        jnp.where(pair_match, jnp.where(source_rows, row_lse[None, :], col_lse[None, :]), 0.0),
        axis=1,
    )
    other_lse = jnp.where(source_rows, col_lse[None, :], row_lse[None, :])
    grad_coeff = loss_scale / pair_count
    grad_scores = grad_coeff * (
        jnp.exp(own_scores - own_lse[:, None])
        + jnp.exp(own_scores - other_lse)
        - 2.0 * pair_match.astype(jnp.float32)
    )
    grad_low = grad_scores.astype(jnp.bfloat16)
    grad_unit = score_scale * jnp.where(
        source_rows, product(grad_low, targets), product(grad_low, sources)
    )
    grad_pooled = own_inverse * (
        grad_unit - own_unit * jnp.sum(grad_unit * own_unit, axis=-1, keepdims=True)
    )
    return (loss_value, grad_pooled)


def gather_units(own, core, me):
    if lax.axis_size("dp") != 16:
        return lax.all_gather(own, ("dp", "tensor"), axis=0, tiled=True)
    mine = place_rows(gather_pieces(own, ALONG_Z, IN_PLANE), ALONG_Z, IN_PLANE, me)
    other = swap_cores(mine)
    rows = own.shape[0]
    parts = both_cores(mine.reshape(16, rows, D), other.reshape(16, rows, D), core, 1)
    return parts.reshape(32 * rows, D)


def gather_full(shard, me):
    if lax.axis_size("dp") != 16:
        return lax.all_gather(shard, "dp", axis=0, tiled=True)
    return place_rows(gather_pieces(shard, ALONG_Z, IN_PLANE), ALONG_Z, IN_PLANE, me)


def reduce_full(partial, me):
    if lax.axis_size("dp") != 16:
        return lax.psum_scatter(partial.astype(f32), "dp", scatter_dimension=0, tiled=True)
    slabs = split_rows(partial.astype(bf16), IN_PLANE, ALONG_Z, me)
    return reduce_pieces(slabs, IN_PLANE, ALONG_Z)


def own_half(array, index, axis=0):
    size = array.shape[axis] // 2
    return lax.dynamic_slice_in_dim(array, index * size, size, axis)


def both_cores(own, other, core, axis):
    left = jnp.where(core == 0, own, other)
    right = jnp.where(core == 0, other, own)
    return jnp.concatenate([left, right], axis=axis)


def local(
    tokens, query_weight, key_weight, value_weight, output_weight, up_weight, down_weight,
    query_bias, value_bias, output_bias, first_gain, first_shift, up_bias, down_bias,
    second_gain, second_shift, group_sizes, sentence_order,
):
    core = lax.axis_index("tensor")
    dp_index = lax.axis_index("dp")
    me = dp_index.astype(jnp.int32).reshape(1)
    head_cols = query_weight.shape[1]
    hidden_cols = up_weight.shape[1]
    qkv_shard = jnp.concatenate([query_weight, key_weight, value_weight], axis=1)
    out_up_shard = jnp.concatenate([output_weight, up_weight], axis=1)
    full_qkv = gather_full(qkv_shard, me)
    full_out_up = gather_full(out_up_shard, me)
    down_own = gather_full(down_weight, me)
    out_up_other = swap_cores(full_out_up)
    down_other = swap_cores(down_own)
    out_own, up_own = full_out_up[:, :head_cols], full_out_up[:, head_cols:]
    out_other, up_other = out_up_other[:, :head_cols], out_up_other[:, head_cols:]
    full_up = both_cores(up_own, up_other, core, 1)
    full_down = both_cores(down_own, down_other, core, 1)
    up_bias_other = swap_cores(up_bias)
    full_up_bias = both_cores(up_bias, up_bias_other, core, 0)

    row_count = tokens.shape[0]
    sentences = row_count // SEQ
    head_shape = (sentences, SEQ, head_cols // HD, HD)
    attn_scale = HD ** (-0.5)
    projected = product(tokens, full_qkv)
    queries = (projected[:, :head_cols] + query_bias).astype(bf16)
    key_rows = projected[:, head_cols : 2 * head_cols].astype(bf16)
    values = (projected[:, 2 * head_cols :] + value_bias).astype(bf16)
    query_heads = queries.reshape(head_shape)
    key_heads = key_rows.reshape(head_shape)
    value_heads = values.reshape(head_shape)
    scores = (
        jnp.einsum("sqhd,skhd->shqk", query_heads, key_heads, preferred_element_type=f32) * attn_scale
    )
    row_peak = jnp.max(scores, axis=-1, keepdims=True)
    log_norm = row_peak + jnp.log(jnp.sum(jnp.exp(scores - row_peak), axis=-1, keepdims=True))
    probs = jnp.exp(scores - log_norm)
    probs_low = probs.astype(bf16)
    context = jnp.einsum("shqk,skhd->sqhd", probs_low, value_heads, preferred_element_type=f32)
    context = context.astype(bf16).reshape(row_count, head_cols)

    context_own = own_half(context, core)
    context_other = swap_cores(own_half(context, 1 - core))
    my_tokens = own_half(tokens, core)
    attended = contract_last(context_own, out_own) + contract_last(context_other, out_other)
    residual = my_tokens.astype(f32) + attended + output_bias
    hidden_first, normed_first, inv_first = norm_forward(residual, first_gain, first_shift)
    hidden_low = hidden_first.astype(bf16)
    pre_act = product(hidden_low, full_up) + full_up_bias
    activation, gelu_back = jax.vjp(exact_gelu, pre_act)
    act_low = activation.astype(bf16)
    second = hidden_first + contract_last(act_low, full_down) + down_bias
    output, normed_two, inv_two = norm_forward(second, second_gain, second_shift)
    my_sentences = sentences // 2
    pooled = jnp.mean(output.reshape(my_sentences, SEQ, D), axis=1)
    pooled_low = (
        pooled * lax.rsqrt(jnp.sum(pooled * pooled, axis=-1, keepdims=True) + norm_eps)
    ).astype(bf16)
    unit_low = gather_units(pooled_low, core, me)
    device = dp_index * 2 + core
    loss_value, grad_pooled = pair_objective(unit_low, pooled, group_sizes, sentence_order, device)
    grad_output = jnp.broadcast_to((grad_pooled / SEQ)[:, None, :], (my_sentences, SEQ, D)).reshape(
        row_count // 2, D
    )
    grad_second, grad_second_gain, grad_second_shift = norm_backward(
        grad_output, normed_two, inv_two, second_gain
    )
    grad_down_bias = jnp.sum(grad_second, axis=0)
    grad_ffn_low = grad_second.astype(bf16)
    grad_down_weight = contract_first(grad_ffn_low, act_low)
    (grad_pre,) = gelu_back(product(grad_ffn_low, full_down))
    grad_pre_low = grad_pre.astype(bf16)
    grad_up_bias = jnp.sum(grad_pre_low.astype(f32), axis=0)
    grad_up_weight = contract_first(hidden_low, grad_pre_low)
    grad_hidden = grad_second + contract_last(grad_pre_low, full_up)
    grad_residual, grad_first_gain, grad_first_shift = norm_backward(
        grad_hidden, normed_first, inv_first, first_gain
    )
    grad_output_bias = jnp.sum(grad_residual, axis=0)
    grad_attn_low = grad_residual.astype(bf16)
    grad_output_own = contract_first(grad_attn_low, context_own)
    grad_output_other = contract_first(grad_attn_low, context_other)
    grad_context_own = product(grad_attn_low, out_own).astype(bf16)
    grad_context_other = swap_cores(product(grad_attn_low, out_other).astype(bf16))
    grad_context = both_cores(grad_context_own, grad_context_other, core, 0).reshape(head_shape)

    def chip_sum(own, other):
        return own + swap_cores(other.astype(bf16)).astype(f32)

    shard_down = reduce_full(chip_sum(own_half(grad_down_weight, core, 1), own_half(grad_down_weight, 1 - core, 1)), me)
    shard_up = reduce_full(chip_sum(own_half(grad_up_weight, core, 1), own_half(grad_up_weight, 1 - core, 1)), me)
    shard_output = reduce_full(chip_sum(grad_output_own, grad_output_other), me)

    grad_values = jnp.einsum("shqk,sqhd->skhd", probs_low, grad_context, preferred_element_type=f32)
    grad_values = grad_values.astype(bf16).reshape(row_count, head_cols)
    grad_probs = jnp.einsum("sqhd,skhd->shqk", grad_context, value_heads, preferred_element_type=f32)
    grad_scores = probs * (grad_probs - jnp.sum(grad_probs * probs, axis=-1, keepdims=True))
    grad_scores_low = grad_scores.astype(bf16)
    grad_queries = jnp.einsum("shqk,skhd->sqhd", grad_scores_low, key_heads, preferred_element_type=f32)
    grad_queries = (grad_queries * attn_scale).astype(bf16).reshape(row_count, head_cols)
    grad_keys = jnp.einsum("shqk,sqhd->skhd", grad_scores_low, query_heads, preferred_element_type=f32)
    grad_keys = (grad_keys * attn_scale).astype(bf16).reshape(row_count, head_cols)
    grad_query_bias = jnp.sum(grad_queries.astype(f32), axis=0)
    grad_value_bias = jnp.sum(grad_values.astype(f32), axis=0)
    grad_qkv = jnp.concatenate([grad_queries, grad_keys, grad_values], axis=1)
    grad_qkv_weight = contract_first(tokens, grad_qkv)
    shard_qkv = reduce_full(grad_qkv_weight, me)
    shard_query = shard_qkv[:, :head_cols]
    shard_key = shard_qkv[:, head_cols : 2 * head_cols]
    shard_value = shard_qkv[:, 2 * head_cols :]
    input_terms = contract_last(grad_qkv, full_qkv)
    my_grad = grad_residual + own_half(input_terms, core) + swap_cores(
        own_half(input_terms, 1 - core).astype(bf16)
    ).astype(f32)
    grad_tokens = both_cores(my_grad, swap_cores(my_grad), core, 0)

    chip_vectors = jnp.concatenate(
        [grad_output_bias, grad_first_gain, grad_first_shift, grad_down_bias, grad_second_gain, grad_second_shift]
    )
    chip_vectors = chip_vectors + swap_cores(chip_vectors)
    up_vector = own_half(grad_up_bias, core) + swap_cores(own_half(grad_up_bias, 1 - core))
    vectors = jnp.concatenate([chip_vectors, up_vector, grad_query_bias, grad_value_bias])
    if lax.axis_size("dp") != 16:
        vectors = lax.psum(vectors, "dp")
    else:
        vectors = sum_small(vectors)
    (
        sum_output_bias, sum_first_gain, sum_first_shift, sum_down_bias, sum_second_gain, sum_second_shift,
        sum_up_bias, sum_query_bias, sum_value_bias,
    ) = jnp.split(
        vectors, [D, 2 * D, 3 * D, 4 * D, 5 * D, 6 * D, 6 * D + hidden_cols, 6 * D + hidden_cols + head_cols]
    )
    return (
        loss_value, grad_tokens, shard_query, shard_key, shard_value, shard_output, shard_up, shard_down,
        sum_query_bias, sum_value_bias, sum_output_bias, sum_first_gain, sum_first_shift, sum_up_bias,
        sum_down_bias, sum_second_gain, sum_second_shift,
    )


def solution(mesh):
    placed = (
        P("dp", None),
        P("dp", "tensor"),
        P("dp", "tensor"),
        P("dp", "tensor"),
        P("dp", "tensor"),
        P("dp", "tensor"),
        P("dp", "tensor"),
        P("tensor"),
        P("tensor"),
        P(),
        P(),
        P(),
        P("tensor"),
        P(),
        P(),
        P(),
        P(),
        P(),
    )
    return jax.shard_map(
        local,
        mesh=mesh,
        in_specs=placed,
        out_specs=(
            P(),
            P("dp", None),
            P("dp", "tensor"),
            P("dp", "tensor"),
            P("dp", "tensor"),
            P("dp", "tensor"),
            P("dp", "tensor"),
            P("dp", "tensor"),
            P("tensor"),
            P("tensor"),
            P(),
            P(),
            P(),
            P("tensor"),
            P(),
            P(),
            P(),
        ),
        check_vma=False,
    )
```

```python
import functools

import jax
import jax.numpy as jnp
from jax import lax
from jax.experimental import pallas as pl
from jax.experimental.pallas import tpu as pltpu
from jax.sharding import PartitionSpec as P

D = 768
HD = 64
SEQ = 64

score_scale = 40.0
margin = 0.3
loss_scale = 65536.0
norm_eps = 1e-06
masked_score = -30000.0

bf16 = jnp.bfloat16
f32 = jnp.float32

ALONG_Z = (4, 8, 12)
IN_PLANE = (1, 2, 3)


def contract(left, right, left_dim, right_dim):
    return lax.dot_general(
        left, right, (((left_dim,), (right_dim,)), ((), ())), preferred_element_type=f32
    )


def product(left, right):
    return contract(left, right, 1, 0)


def contract_last(left, right):
    return contract(left, right, 1, 1)


def contract_first(left, right):
    return contract(left, right, 0, 0)


def swap_cores(array):
    return lax.ppermute(array, "tensor", [(0, 1), (1, 0)])


def swap_chips(array, mask):
    count = lax.axis_size("dp")
    return lax.ppermute(array, "dp", [(i, i ^ mask) for i in range(count)])


def rows_orders(dp):
    if dp != 16:
        return ((0,), (0,))
    return tuple(tuple(j ^ i for j in plane for i in (0, *ALONG_Z)) for plane in ((0, 1, 2, 3), (0, 2, 1, 3)))


def gather_rows(shard, split):
    if lax.axis_size("dp") != 16:
        full = lax.all_gather(shard, "dp", axis=0, tiled=True)
        return full[:, :split], full[:, split:]
    near = jnp.concatenate([shard] + [swap_chips(shard, mask) for mask in ALONG_Z], axis=0)
    near_a, near_b = near[:, :split], near[:, split:]
    low_a = jnp.concatenate([near_a, swap_chips(near_a, 1)], axis=0)
    low_b = jnp.concatenate([near_b, swap_chips(near_b, 2)], axis=0)
    return (
        jnp.concatenate([low_a, swap_chips(low_a, 2)], axis=0),
        jnp.concatenate([low_b, swap_chips(low_b, 1)], axis=0),
    )


def reduce_rows(part_a, part_b):
    if lax.axis_size("dp") != 16:
        both = jnp.concatenate([part_a, part_b], axis=1).astype(f32)
        return lax.psum_scatter(both, "dp", scatter_dimension=0, tiled=True)

    def halve(array, mask):
        rows = array.shape[0] // 2
        return (array[:rows].astype(f32) + swap_chips(array[rows:], mask).astype(f32)).astype(bf16)

    part_a, part_b = halve(part_a, 2), halve(part_b, 1)
    part_a, part_b = halve(part_a, 1), halve(part_b, 2)
    near = jnp.concatenate([part_a, part_b], axis=1)
    rows = near.shape[0] // 4
    total = near[:rows].astype(f32)
    for i, mask in enumerate(ALONG_Z):
        total = total + swap_chips(near[(i + 1) * rows : (i + 2) * rows], mask).astype(f32)
    return total


def gather_units(own):
    if lax.axis_size("dp") != 16:
        mine = lax.all_gather(own, "dp", axis=0, tiled=True)
    else:
        near = jnp.concatenate([own] + [swap_chips(own, mask) for mask in ALONG_Z], axis=0)
        mine = jnp.concatenate([near] + [swap_chips(near, mask) for mask in IN_PLANE], axis=0)
    return mine, swap_cores(mine)


def sum_small(array):
    if lax.axis_size("dp") != 16:
        return lax.psum(array, "dp")
    for group in (ALONG_Z, IN_PLANE):
        a, b, c = [swap_chips(array, mask) for mask in group]
        array = (array + a) + (b + c)
    return array


def column_mask():
    row = lax.broadcasted_iota(jnp.int32, (2 * SEQ, 2 * HD), 0) // SEQ
    column = lax.broadcasted_iota(jnp.int32, (2 * SEQ, 2 * HD), 1) // HD
    return (row == column).astype(f32).astype(bf16)


def two_heads(pair, mask):
    return jnp.concatenate([pair, pair], axis=0) * mask


def pick_heads(both, first):
    return jnp.where(first, both[:SEQ], both[SEQ:])


def block_copies(source, target, order, me, sem):
    rows = source.shape[0] // len(order)
    copies = []
    for k, mask in enumerate(order):
        to = pl.multiple_of((me ^ mask) * rows, 16) if len(order) > 1 else 0
        copies.append(
            pltpu.make_async_copy(source.at[pl.ds(k * rows, rows)], target.at[pl.ds(to, rows)], sem)
        )
    return copies


def start_all(copies):
    for copy in copies:
        copy.start()


def wait_whole(target, sem):
    pltpu.make_async_copy(target, target, sem).wait()


def attention_forward_kernel(
    orders, where_ref, tokens_ref, query_bias_ref, value_bias_ref, part_a, part_b,
    query_ref, key_ref, value_ref, context_ref, probs_ref, weight, sem,
):
    width_a = part_a.shape[1]
    head_cols = query_ref.shape[1]

    @pl.when(pl.program_id(0) == 0)
    def _():
        me = where_ref[0]
        start_all(block_copies(part_a, weight.at[:, pl.ds(0, width_a)], orders[0], me, sem.at[0]))
        start_all(block_copies(part_b, weight.at[:, pl.ds(width_a, part_b.shape[1])], orders[1], me, sem.at[0]))
        wait_whole(weight, sem.at[0])

    rows = tokens_ref.shape[0]
    projected = product(tokens_ref[...], weight[...])
    query_ref[...] = (projected[:, :head_cols] + query_bias_ref[...]).astype(bf16)
    key_ref[...] = projected[:, head_cols : 2 * head_cols].astype(bf16)
    value_ref[...] = (projected[:, 2 * head_cols :] + value_bias_ref[...]).astype(bf16)
    mask = column_mask()
    first = lax.broadcasted_iota(jnp.int32, (SEQ, 2 * HD), 1) < HD
    for sentence in range(rows // SEQ):
        at = slice(sentence * SEQ, (sentence + 1) * SEQ)
        for pair in range(head_cols // (2 * HD)):
            columns = slice(pair * 2 * HD, (pair + 1) * 2 * HD)
            scores = contract_last(key_ref[at, columns], two_heads(query_ref[at, columns], mask)) * HD ** (-0.5)
            powers = jnp.exp(scores - jnp.max(scores, axis=0, keepdims=True))
            probs = powers / jnp.sum(powers, axis=0, keepdims=True)
            probs_ref[at, columns] = probs
            both = contract_first(probs.astype(bf16), value_ref[at, columns])
            context_ref[at, columns] = pick_heads(both, first).astype(bf16)


def any_spec():
    return pl.BlockSpec(memory_space=pl.ANY)


def whole_spec(shape):
    return pl.BlockSpec(shape, lambda *_: (0,) * len(shape), pipeline_mode=pl.Buffered(1))


def kernel_params():
    return pltpu.CompilerParams(vmem_limit_bytes=60 * 1024 * 1024, dimension_semantics=("arbitrary",))


def attention_forward(orders, where, tokens, query_bias, value_bias, part_a, part_b):
    rows = tokens.shape[0]
    head_cols = query_bias.shape[1]
    block = 4 * SEQ
    by_rows = lambda i, where: (i, 0)
    out = lambda dtype: jax.ShapeDtypeStruct((rows, head_cols), dtype)
    return pl.pallas_call(
        functools.partial(attention_forward_kernel, orders),
        out_shape=[out(bf16)] * 4 + [out(f32)],
        grid_spec=pltpu.PrefetchScalarGridSpec(
            num_scalar_prefetch=1,
            grid=(rows // block,),
            in_specs=[
                pl.BlockSpec((block, D), by_rows),
                whole_spec((1, head_cols)), whole_spec((1, head_cols)), any_spec(), any_spec(),
            ],
            out_specs=[pl.BlockSpec((block, head_cols), by_rows)] * 5,
            scratch_shapes=[pltpu.VMEM((D, 3 * head_cols), bf16), pltpu.SemaphoreType.DMA((1,))],
        ),
        compiler_params=kernel_params(),
        cost_estimate=pl.CostEstimate(
            flops=2 * rows * D * 3 * head_cols * 2, bytes_accessed=rows * head_cols * 30, transcendentals=0
        ),
        name="attention_forward",
    )(where, tokens, query_bias, value_bias, part_a, part_b)


TAIL = (0.1167079709, 0.07627463045, 0.2455670143, -0.1994404095, 0.3630729868, -0.1021822206)


def normal_parts(values):
    bell = jnp.exp(values * values * -0.5)
    ratio = 1.0 / (1.0 + (0.4 * 0.5**0.5) * jnp.abs(values))
    tail = jnp.full_like(values, TAIL[5])
    for factor in TAIL[4::-1]:
        tail = tail * ratio + factor
    tail = tail * ratio * bell
    return jnp.where(values < 0.0, tail, 1.0 - tail), bell * 0.3989422804014327


def feed_forward_kernel(
    orders, where_ref, tokens_ref, context_own_ref, context_other_ref, output_bias_ref, gain_one_ref, shift_one_ref,
    up_bias_own_ref, up_bias_other_ref, down_bias_ref, gain_two_ref, shift_two_ref,
    up_own_a, up_own_b, up_other_a, up_other_b, down_own_a, down_own_b, down_other_a, down_other_b,
    hidden_ref, normed_one_ref, inv_one_ref, act_ref, slope_ref, normed_two_ref, inv_two_ref, pooled_ref, unit_ref,
    out_up, down, sem,
):
    head_cols = context_own_ref.shape[1]
    hidden_cols = up_bias_own_ref.shape[1]

    @pl.when(pl.program_id(0) == 0)
    def _():
        me = where_ref[0]
        for half, (part_a, part_b) in enumerate(((up_own_a, up_own_b), (up_other_a, up_other_b))):
            at = out_up.at[half]
            start_all(block_copies(part_a, at.at[:, pl.ds(0, part_a.shape[1])], orders[0], me, sem.at[half]))
            start_all(block_copies(part_b, at.at[:, pl.ds(part_a.shape[1], part_b.shape[1])], orders[1], me, sem.at[half]))
        for half, (part_a, part_b) in enumerate(((down_own_a, down_own_b), (down_other_a, down_other_b))):
            at = down.at[half]
            start_all(block_copies(part_a, at.at[:, pl.ds(0, part_a.shape[1])], orders[0], me, sem.at[2 + half]))
            start_all(block_copies(part_b, at.at[:, pl.ds(part_a.shape[1], part_b.shape[1])], orders[1], me, sem.at[2 + half]))
        for half in range(2):
            wait_whole(out_up.at[half], sem.at[half])
            wait_whole(down.at[half], sem.at[2 + half])

    attended = contract_last(context_own_ref[...], out_up[0, :, :head_cols]) + contract_last(
        context_other_ref[...], out_up[1, :, :head_cols]
    )
    residual = tokens_ref[...].astype(f32) + attended + output_bias_ref[...]
    centred = residual - jnp.mean(residual, axis=1, keepdims=True)
    inv_one = lax.rsqrt(jnp.mean(centred * centred, axis=1, keepdims=True) + norm_eps)
    normed = centred * inv_one
    normed_one_ref[...] = normed.astype(bf16)
    inv_one_ref[...] = inv_one
    hidden = normed * gain_one_ref[...] + shift_one_ref[...]
    hidden_low = hidden.astype(bf16)
    hidden_ref[...] = hidden_low
    second = hidden + down_bias_ref[...]
    step = 512
    for half, bias_ref in enumerate((up_bias_own_ref, up_bias_other_ref)):
        for start in range(0, hidden_cols, step):
            columns = slice(start, start + step)
            pre_act = product(hidden_low, out_up[half, :, head_cols + start : head_cols + start + step])
            pre_act = pre_act + bias_ref[:, columns]
            below, density = normal_parts(pre_act)
            act = (pre_act * below).astype(bf16)
            to = slice(half * hidden_cols + start, half * hidden_cols + start + step)
            act_ref[:, to] = act
            slope_ref[:, to] = (below + pre_act * density).astype(bf16)
            second = second + contract_last(act, down[half, :, columns])
    centred = second - jnp.mean(second, axis=1, keepdims=True)
    inv_two = lax.rsqrt(jnp.mean(centred * centred, axis=1, keepdims=True) + norm_eps)
    normed = centred * inv_two
    normed_two_ref[...] = normed.astype(bf16)
    inv_two_ref[...] = inv_two
    output = normed * gain_two_ref[...] + shift_two_ref[...]
    count = output.shape[0] // SEQ
    pooled = jnp.concatenate(
        [jnp.mean(output[s * SEQ : (s + 1) * SEQ], axis=0, keepdims=True) for s in range(count)], axis=0
    )
    unit = pooled * lax.rsqrt(jnp.sum(pooled * pooled, axis=1, keepdims=True) + norm_eps)
    pooled_ref[0] = pooled
    unit_ref[0] = unit.astype(bf16).astype(f32)


def feed_forward(orders, where, tokens, context, context_other, vectors, parts):
    rows = tokens.shape[0] // 2
    head_cols = context.shape[1]
    hidden_cols = vectors[3].shape[1]
    block = 4 * SEQ
    blocks = rows // block
    by_rows = lambda i, where: (i, 0)
    mine = lambda i, where: (where[1] * blocks + i, 0)
    out = lambda width, dtype: jax.ShapeDtypeStruct((rows, width), dtype)
    pooled_shape = jax.ShapeDtypeStruct((blocks, block // SEQ, D), f32)
    pooled_spec = pl.BlockSpec((1, block // SEQ, D), lambda i, where: (i, 0, 0))
    return pl.pallas_call(
        functools.partial(feed_forward_kernel, orders),
        out_shape=[
            out(D, bf16), out(D, bf16), out(1, f32), out(2 * hidden_cols, bf16), out(2 * hidden_cols, bf16),
            out(D, bf16), out(1, f32), pooled_shape, pooled_shape,
        ],
        grid_spec=pltpu.PrefetchScalarGridSpec(
            num_scalar_prefetch=1,
            grid=(blocks,),
            in_specs=[
                pl.BlockSpec((block, D), mine), pl.BlockSpec((block, head_cols), mine),
                pl.BlockSpec((block, head_cols), by_rows),
            ]
            + [whole_spec(vector.shape) for vector in vectors]
            + [any_spec()] * 8,
            out_specs=[
                pl.BlockSpec((block, D), by_rows), pl.BlockSpec((block, D), by_rows), pl.BlockSpec((block, 1), by_rows),
                pl.BlockSpec((block, 2 * hidden_cols), by_rows), pl.BlockSpec((block, 2 * hidden_cols), by_rows),
                pl.BlockSpec((block, D), by_rows), pl.BlockSpec((block, 1), by_rows), pooled_spec, pooled_spec,
            ],
            scratch_shapes=[
                pltpu.VMEM((2, D, head_cols + hidden_cols), bf16), pltpu.VMEM((2, D, hidden_cols), bf16),
                pltpu.SemaphoreType.DMA((4,)),
            ],
        ),
        compiler_params=kernel_params(),
        cost_estimate=pl.CostEstimate(
            flops=2 * rows * D * 2 * (2 * hidden_cols + head_cols), bytes_accessed=30_000_000, transcendentals=0
        ),
        name="feed_forward",
    )(where, tokens, context, context_other, *vectors, *parts)


def pair_kernel(
    order, where_ref, sizes_ref, own_ref, other_ref, pooled_ref, order_row_ref, order_column_ref,
    loss_ref, grad_ref, units, coeffs,
):
    me, core = where_ref[0], where_ref[1]
    count = units.shape[0]
    pairs = count // 2
    rows = own_ref.shape[0] // len(order)
    for k, mask in enumerate(order):
        at = slice(k * rows, (k + 1) * rows)
        units[pl.ds(pl.multiple_of(((me ^ mask) * 2 + core) * rows, 16), rows), :] = own_ref[at, :]
        units[pl.ds(pl.multiple_of(((me ^ mask) * 2 + 1 - core) * rows, 16), rows), :] = other_ref[at, :]
    along_rows = lax.broadcasted_iota(jnp.int32, (count, count), 0)
    along_columns = lax.broadcasted_iota(jnp.int32, (count, count), 1)
    place_column = jnp.sum(jnp.where(order_row_ref[...] == along_rows, along_columns, 0), axis=1, keepdims=True)
    place_row = jnp.sum(jnp.where(order_column_ref[...] == along_columns, along_rows, 0), axis=0, keepdims=True)

    def describe(place):
        source = (place < pairs).astype(jnp.int32)
        pair = place - pairs * (1 - source)
        group = jnp.zeros_like(pair)
        end = jnp.int32(0)
        for g in range(sizes_ref.shape[0]):
            end = end + sizes_ref[g]
            group = group + (pair >= end).astype(jnp.int32)
        return source, pair, group

    source_column, pair_column, group_column = describe(place_column)
    source_row, pair_row, group_row = describe(place_row)
    across = source_column != source_row
    partner = across & (pair_column == pair_row)
    scores = score_scale * contract_last(units[...], units[...])
    scores = scores - score_scale * margin * partner.astype(f32)
    scores = jnp.where(across & (group_column == group_row), scores, masked_score)

    def log_total(axis):
        peak = jnp.max(scores, axis=axis, keepdims=True)
        return peak + jnp.log(jnp.sum(jnp.exp(scores - peak), axis=axis, keepdims=True))

    lse_column, lse_row = log_total(1), log_total(0)
    matched = jnp.sum(jnp.where(partner, scores, 0.0), axis=1, keepdims=True)
    loss = jnp.sum(lse_column - matched, axis=0, keepdims=True) * (1.0 / pairs)
    loss_ref[...] = jnp.broadcast_to(loss, loss_ref.shape)
    coeffs[...] = (loss_scale / pairs) * (
        jnp.exp(scores - lse_column) + jnp.exp(scores - lse_row) - 2.0 * partner.astype(f32)
    )
    mine = pl.ds(pl.multiple_of((me * 2 + core) * rows, 16), rows)
    grad_unit = score_scale * product(coeffs[mine, :].astype(bf16), units[...])
    pooled = pooled_ref[...]
    inverse = lax.rsqrt(jnp.sum(pooled * pooled, axis=1, keepdims=True) + norm_eps)
    unit = pooled * inverse
    grad_ref[...] = inverse * (grad_unit - unit * jnp.sum(grad_unit * unit, axis=1, keepdims=True))


def pair_gradient(order, where, group_sizes, sentence_order, own, other, pooled):
    count = sentence_order.shape[0]
    return pl.pallas_call(
        functools.partial(pair_kernel, order),
        out_shape=[jax.ShapeDtypeStruct((8, 128), f32), jax.ShapeDtypeStruct(pooled.shape, f32)],
        grid_spec=pltpu.PrefetchScalarGridSpec(
            num_scalar_prefetch=2,
            grid=(1,),
            in_specs=[
                whole_spec(own.shape), whole_spec(other.shape), whole_spec(pooled.shape),
                whole_spec((1, count)), whole_spec((count, 1)),
            ],
            out_specs=[whole_spec((8, 128)), whole_spec(pooled.shape)],
            scratch_shapes=[pltpu.VMEM((count, D), bf16), pltpu.VMEM((count, count), f32)],
        ),
        compiler_params=kernel_params(),
        cost_estimate=pl.CostEstimate(flops=2 * count * count * D, bytes_accessed=2_000_000, transcendentals=0),
        name="pair_gradient",
    )(where, group_sizes, own, other, pooled, sentence_order.reshape(1, count), sentence_order.reshape(count, 1))


def turn_rows(values, orders, me, turned, target_a, target_b):
    turned[...] = values.T
    for order, target in ((orders[0], target_a), (orders[1], target_b)):
        rows = turned.shape[0] // len(order)
        for k, mask in enumerate(order):
            at = pl.multiple_of((me ^ mask) * rows, 16) if len(order) > 1 else 0
            target[k * rows : (k + 1) * rows, :] = turned[pl.ds(at, rows), :]


def down_gradient_kernel(
    orders, where_ref, grad_pooled_ref, normed_ref, inv_ref, gain_ref, act_ref,
    second_ref, low_ref, weight_ref, sums_ref, turned, turned_both,
):
    @pl.when(pl.program_id(0) == 0)
    def _():
        gain = gain_ref[...]
        gain_sum = jnp.zeros((1, D), f32)
        shift_sum = jnp.zeros((1, D), f32)
        bias_sum = jnp.zeros((1, D), f32)
        for sentence in range(grad_pooled_ref.shape[0]):
            at = slice(sentence * SEQ, (sentence + 1) * SEQ)
            upstream = grad_pooled_ref[sentence : sentence + 1, :] * (1.0 / SEQ)
            scaled = upstream * gain
            normed = normed_ref[at, :].astype(f32)
            second_mean = jnp.mean(scaled * normed, axis=1, keepdims=True)
            grad = inv_ref[at, :] * (scaled - jnp.mean(scaled, axis=1, keepdims=True) - normed * second_mean)
            second_ref[at, :] = grad
            low_ref[at, :] = grad.astype(bf16)
            gain_sum = gain_sum + upstream * jnp.sum(normed, axis=0, keepdims=True)
            shift_sum = shift_sum + upstream * SEQ
            bias_sum = bias_sum + jnp.sum(grad, axis=0, keepdims=True)
        sums_ref[0:1, :] = gain_sum
        sums_ref[1:2, :] = shift_sum
        sums_ref[2:3, :] = bias_sum
        turn_rows(low_ref[...], orders, where_ref[0], turned, turned_both.at[0], turned_both.at[1])

    which = lax.rem(pl.program_id(0), 2)
    weight_ref[0] = product(turned_both[which], act_ref[...]).astype(bf16)


def down_gradient(orders, where, grad_pooled, normed, inv, gain, act):
    rows, hidden = act.shape
    chunk = hidden // 4
    return pl.pallas_call(
        functools.partial(down_gradient_kernel, orders),
        out_shape=[
            jax.ShapeDtypeStruct((rows, D), f32), jax.ShapeDtypeStruct((rows, D), bf16),
            jax.ShapeDtypeStruct((4, D, chunk), bf16), jax.ShapeDtypeStruct((8, D), f32),
        ],
        grid_spec=pltpu.PrefetchScalarGridSpec(
            num_scalar_prefetch=1,
            grid=(4,),
            in_specs=[
                whole_spec(grad_pooled.shape), whole_spec((rows, D)), whole_spec((rows, 1)), whole_spec((1, D)),
                pl.BlockSpec((rows, chunk), lambda i, where: (0, i)),
            ],
            out_specs=[
                whole_spec((rows, D)), whole_spec((rows, D)),
                pl.BlockSpec((1, D, chunk), lambda i, where: (i, 0, 0)), whole_spec((8, D)),
            ],
            scratch_shapes=[pltpu.VMEM((D, rows), bf16), pltpu.VMEM((2, D, rows), bf16)],
        ),
        compiler_params=kernel_params(),
        cost_estimate=pl.CostEstimate(flops=2 * rows * D * hidden, bytes_accessed=20_000_000, transcendentals=0),
        name="down_gradient",
    )(where, grad_pooled, normed, inv, gain, act)


def up_gradient_kernel(
    orders, where_ref, second_ref, low_ref, slope_ref, hidden_ref, normed_ref, inv_ref, gain_ref,
    context_own_ref, context_other_ref,
    up_own_a, up_own_b, up_other_a, up_other_b, down_own_a, down_own_b, down_other_a, down_other_b,
    weight_ref, bias_ref, residual_ref, context_grad_own_ref, context_grad_other_ref, out_weight_ref, sums_ref,
    out_up, down, total, attn_low, turned, turned_both, sem,
):
    me = where_ref[0]
    step = pl.program_id(0)
    head_cols = context_own_ref.shape[1]
    chunk = slope_ref.shape[1]

    @pl.when(step == 0)
    def _():
        for half, (part_a, part_b) in enumerate(((up_own_a, up_own_b), (up_other_a, up_other_b))):
            at = out_up.at[half]
            start_all(block_copies(part_a, at.at[:, pl.ds(0, part_a.shape[1])], orders[0], me, sem.at[half]))
            start_all(block_copies(part_b, at.at[:, pl.ds(part_a.shape[1], part_b.shape[1])], orders[1], me, sem.at[half]))
        for half, (part_a, part_b) in enumerate(((down_own_a, down_own_b), (down_other_a, down_other_b))):
            at = down.at[half]
            start_all(block_copies(part_a, at.at[:, pl.ds(0, part_a.shape[1])], orders[0], me, sem.at[2 + half]))
            start_all(block_copies(part_b, at.at[:, pl.ds(part_a.shape[1], part_b.shape[1])], orders[1], me, sem.at[2 + half]))
        turn_rows(hidden_ref[...], orders, me, turned, turned_both.at[0], turned_both.at[1])
        total[...] = second_ref[...]
        for half in range(2):
            wait_whole(out_up.at[half], sem.at[half])
            wait_whole(down.at[half], sem.at[2 + half])

    half, which = step // 2, lax.rem(step, 2)
    grad_act = product(low_ref[...], down[half, :, pl.ds(pl.multiple_of(which * chunk, 128), chunk)])
    grad_pre = (grad_act * slope_ref[...].astype(f32)).astype(bf16)
    bias_ref[0] = jnp.broadcast_to(jnp.sum(grad_pre.astype(f32), axis=0, keepdims=True), bias_ref.shape[1:])
    weight_ref[0] = product(turned_both[which], grad_pre).astype(bf16)
    total[...] += contract_last(grad_pre, out_up[half, :, pl.ds(pl.multiple_of(head_cols + which * chunk, 128), chunk)])

    @pl.when(step == 3)
    def _():
        gain = gain_ref[...]
        gain_sum = jnp.zeros((1, D), f32)
        shift_sum = jnp.zeros((1, D), f32)
        bias_sum = jnp.zeros((1, D), f32)
        rows = 128
        for start in range(0, total.shape[0], rows):
            at = slice(start, start + rows)
            upstream = total[at, :]
            normed = normed_ref[at, :].astype(f32)
            scaled = upstream * gain
            first_mean = jnp.mean(scaled, axis=1, keepdims=True)
            second_mean = jnp.mean(scaled * normed, axis=1, keepdims=True)
            grad = inv_ref[at, :] * (scaled - first_mean - normed * second_mean)
            residual_ref[at, :] = grad
            low = grad.astype(bf16)
            attn_low[at, :] = low
            gain_sum = gain_sum + jnp.sum(upstream * normed, axis=0, keepdims=True)
            shift_sum = shift_sum + jnp.sum(upstream, axis=0, keepdims=True)
            bias_sum = bias_sum + jnp.sum(grad, axis=0, keepdims=True)
            context_grad_own_ref[at, :] = product(low, out_up[0, :, :head_cols]).astype(bf16)
            context_grad_other_ref[at, :] = product(low, out_up[1, :, :head_cols]).astype(bf16)
        sums_ref[0:1, :] = gain_sum
        sums_ref[1:2, :] = shift_sum
        sums_ref[2:3, :] = bias_sum
        turn_rows(attn_low[...], orders, me, turned, turned_both.at[0], turned_both.at[1])
        split = OUT_SPLIT
        for k, context_ref in enumerate((context_own_ref, context_other_ref)):
            out_weight_ref[k, :, :split] = product(turned_both[0], context_ref[:, :split]).astype(bf16)
            out_weight_ref[k, :, split:] = product(turned_both[1], context_ref[:, split:]).astype(bf16)


OUT_SPLIT = 128


def up_gradient(orders, where, second, low, slope, hidden_low, normed, inv, gain, context, context_other, parts):
    rows, hidden = slope.shape
    head_cols = context.shape[1]
    chunk = hidden // 4
    mine = lambda i, where: (where[1], 0)
    return pl.pallas_call(
        functools.partial(up_gradient_kernel, orders),
        out_shape=[
            jax.ShapeDtypeStruct((4, D, chunk), bf16), jax.ShapeDtypeStruct((4, 8, chunk), f32),
            jax.ShapeDtypeStruct((rows, D), f32),
            jax.ShapeDtypeStruct((rows, head_cols), bf16), jax.ShapeDtypeStruct((rows, head_cols), bf16),
            jax.ShapeDtypeStruct((2, D, head_cols), bf16), jax.ShapeDtypeStruct((8, D), f32),
        ],
        grid_spec=pltpu.PrefetchScalarGridSpec(
            num_scalar_prefetch=1,
            grid=(4,),
            in_specs=[
                whole_spec((rows, D)), whole_spec((rows, D)),
                pl.BlockSpec((rows, chunk), lambda i, where: (0, i)),
                whole_spec((rows, D)), whole_spec((rows, D)), whole_spec((rows, 1)), whole_spec((1, D)),
                pl.BlockSpec((rows, head_cols), mine, pipeline_mode=pl.Buffered(1)), whole_spec((rows, head_cols)),
            ]
            + [any_spec()] * 8,
            out_specs=[
                pl.BlockSpec((1, D, chunk), lambda i, where: (i, 0, 0)),
                pl.BlockSpec((1, 8, chunk), lambda i, where: (i, 0, 0)),
                whole_spec((rows, D)), whole_spec((rows, head_cols)), whole_spec((rows, head_cols)),
                whole_spec((2, D, head_cols)), whole_spec((8, D)),
            ],
            scratch_shapes=[
                pltpu.VMEM((2, D, head_cols + hidden // 2), bf16), pltpu.VMEM((2, D, hidden // 2), bf16),
                pltpu.VMEM((rows, D), f32), pltpu.VMEM((rows, D), bf16), pltpu.VMEM((D, rows), bf16),
                pltpu.VMEM((2, D, rows), bf16), pltpu.SemaphoreType.DMA((4,)),
            ],
        ),
        compiler_params=kernel_params(),
        cost_estimate=pl.CostEstimate(flops=6 * rows * D * hidden, bytes_accessed=40_000_000, transcendentals=0),
        name="up_gradient",
    )(where, second, low, slope, hidden_low, normed, inv, gain, context, context_other, *parts)


def attention_backward_kernel(
    orders, where_ref, tokens_ref, query_ref, key_ref, value_ref, probs_ref, grad_other_ref, grad_own_ref,
    residual_ref, part_a, part_b,
    terms_other_ref, tokens_grad_ref, weight_a_ref, weight_b_ref, bias_ref,
    weight, grads, turned, turned_a, turned_b, sem,
):
    me = where_ref[0]
    step = pl.program_id(0)
    blocks = pl.num_programs(0)
    rows, head_cols = query_ref.shape
    width_a = part_a.shape[1]

    @pl.when(step == 0)
    def _():
        start_all(block_copies(part_a, weight.at[:, pl.ds(0, width_a)], orders[0], me, sem.at[0]))
        start_all(block_copies(part_b, weight.at[:, pl.ds(width_a, part_b.shape[1])], orders[1], me, sem.at[0]))
        bias_ref[...] = jnp.zeros_like(bias_ref)

    at_block = pl.ds(pl.multiple_of(step * rows, rows), rows)
    turn_rows(tokens_ref[...], orders, me, turned, turned_a.at[:, at_block], turned_b.at[:, at_block])
    other = step < blocks // 2
    mask = column_mask()
    first = lax.broadcasted_iota(jnp.int32, (SEQ, 2 * HD), 1) < HD
    scale = HD ** (-0.5)
    for sentence in range(rows // SEQ):
        at = slice(sentence * SEQ, (sentence + 1) * SEQ)
        to = pl.ds(pl.multiple_of(step * rows + sentence * SEQ, SEQ), SEQ)
        for pair in range(head_cols // (2 * HD)):
            columns = slice(pair * 2 * HD, (pair + 1) * 2 * HD)
            upstream = jnp.where(other, grad_other_ref[at, columns], grad_own_ref[at, columns])
            upstream = two_heads(upstream, mask)
            probs = probs_ref[at, columns]
            grad_probs = contract_last(value_ref[at, columns], upstream)
            inner = jnp.sum(grad_probs * probs, axis=0, keepdims=True)
            grad_scores = (probs * (grad_probs - inner)).astype(bf16)
            grad_value = product(probs.astype(bf16), upstream)
            grad_key = product(grad_scores, two_heads(query_ref[at, columns], mask)) * scale
            grad_query = pick_heads(contract_first(grad_scores, key_ref[at, columns]), first) * scale
            for k, grad in enumerate((grad_query, grad_key, grad_value)):
                grads[to, k * head_cols + pair * 2 * HD : k * head_cols + (pair + 1) * 2 * HD] = grad.astype(bf16)

    @pl.when(step == 0)
    def _():
        wait_whole(weight, sem.at[0])

    here = grads[at_block, :]
    bias_ref[...] += jnp.broadcast_to(jnp.sum(here.astype(f32), axis=0, keepdims=True), bias_ref.shape)
    terms = contract_last(here, weight[...])

    @pl.when(other)
    def _():
        terms_other_ref[...] = terms.astype(bf16)

    @pl.when(jnp.logical_not(other))
    def _():
        tokens_grad_ref[...] = terms + residual_ref[...]

    @pl.when(step == blocks - 1)
    def _():
        weight_a_ref[...] = product(turned_a[...], grads[:, :width_a]).astype(bf16)
        weight_b_ref[...] = product(turned_b[...], grads[:, width_a:]).astype(bf16)


def attention_backward(orders, where, tokens, queries, key_rows, values, probs, grad_other, grad_own, residual, part_a, part_b):
    rows = tokens.shape[0]
    head_cols = queries.shape[1]
    block = 4 * SEQ
    half = rows // block // 2
    split, rest = part_a.shape[1], part_b.shape[1]
    by_rows = lambda i, where: (jnp.where(i < half, (1 - where[1]) * half + i, where[1] * half + i - half), 0)
    early = lambda i, where: (jnp.minimum(i, half - 1), 0)
    late = lambda i, where: (jnp.maximum(i - half, 0), 0)
    heads = pl.BlockSpec((block, head_cols), by_rows)
    return pl.pallas_call(
        functools.partial(attention_backward_kernel, orders),
        out_shape=[
            jax.ShapeDtypeStruct((rows // 2, D), bf16), jax.ShapeDtypeStruct((rows // 2, D), f32),
            jax.ShapeDtypeStruct((D, split), bf16), jax.ShapeDtypeStruct((D, rest), bf16),
            jax.ShapeDtypeStruct((8, 3 * head_cols), f32),
        ],
        grid_spec=pltpu.PrefetchScalarGridSpec(
            num_scalar_prefetch=1,
            grid=(2 * half,),
            in_specs=[
                pl.BlockSpec((block, D), by_rows), heads, heads, heads, heads,
                pl.BlockSpec((block, head_cols), early), pl.BlockSpec((block, head_cols), late),
                pl.BlockSpec((block, D), late), any_spec(), any_spec(),
            ],
            out_specs=[
                pl.BlockSpec((block, D), early), pl.BlockSpec((block, D), late),
                whole_spec((D, split)), whole_spec((D, rest)), whole_spec((8, 3 * head_cols)),
            ],
            scratch_shapes=[
                pltpu.VMEM((D, 3 * head_cols), bf16), pltpu.VMEM((rows, 3 * head_cols), bf16),
                pltpu.VMEM((D, block), bf16), pltpu.VMEM((D, rows), bf16), pltpu.VMEM((D, rows), bf16),
                pltpu.SemaphoreType.DMA((1,)),
            ],
        ),
        compiler_params=kernel_params(),
        cost_estimate=pl.CostEstimate(
            flops=2 * rows * D * 3 * head_cols * 2, bytes_accessed=30_000_000, transcendentals=0
        ),
        name="attention_backward",
    )(where, tokens, queries, key_rows, values, probs, grad_other, grad_own, residual, part_a, part_b)


def pair_objective(unit_low, pooled, group_sizes, sentence_order, device):
    total_sent = unit_low.shape[0]
    pair_count = total_sent // 2
    own_count = pooled.shape[0]
    sources = jnp.take(unit_low, sentence_order[:pair_count], axis=0)
    targets = jnp.take(unit_low, sentence_order[pair_count:], axis=0)
    group_ends = jnp.cumsum(group_sizes)
    pair_ids = jnp.arange(pair_count, dtype=jnp.int32)
    group_of = jnp.sum((pair_ids[:, None] >= group_ends[None, :]).astype(jnp.int32), axis=1)
    block_rows = min(512, pair_count)

    def scan_step(carried, offset):
        col_peak, col_total = carried
        row_ids = offset + jnp.arange(block_rows, dtype=jnp.int32)
        row_units = lax.dynamic_slice_in_dim(sources, offset, block_rows, 0)
        row_groups = lax.dynamic_slice_in_dim(group_of, offset, block_rows, 0)
        is_same = row_ids[:, None] == pair_ids[None, :]
        scores = score_scale * contract_last(row_units, targets)
        scores = scores - score_scale * margin * is_same.astype(jnp.float32)
        scores = jnp.where(row_groups[:, None] == group_of[None, :], scores, masked_score)
        row_peak = jnp.max(scores, axis=1, keepdims=True)
        row_lse = row_peak[:, 0] + jnp.log(jnp.sum(jnp.exp(scores - row_peak), axis=1))
        diagonal = jnp.sum(jnp.where(is_same, scores, 0.0), axis=1)
        new_peak = jnp.maximum(col_peak, jnp.max(scores, axis=0))
        new_total = col_total * jnp.exp(col_peak - new_peak) + jnp.sum(
            jnp.exp(scores - new_peak[None, :]), axis=0
        )
        return ((new_peak, new_total), (row_lse, diagonal))

    offsets = jnp.arange(pair_count // block_rows, dtype=jnp.int32) * block_rows
    start_state = (
        jnp.full((pair_count,), -1e30, jnp.float32),
        jnp.zeros((pair_count,), jnp.float32),
    )
    (col_peak, col_total), (row_lse, diagonal) = lax.scan(scan_step, start_state, offsets)
    col_lse = col_peak + jnp.log(col_total)
    row_lse = row_lse.reshape(pair_count)
    diagonal = diagonal.reshape(pair_count)
    loss_value = jnp.mean(row_lse + col_lse - 2.0 * diagonal)
    own_ids = device * own_count + jnp.arange(own_count, dtype=jnp.int32)
    matches = sentence_order[None, :] == own_ids[:, None]
    position = jnp.sum(
        jnp.where(matches, jnp.arange(total_sent, dtype=jnp.int32)[None, :], 0), axis=1
    )
    is_source = position < pair_count
    own_pair = jnp.where(is_source, position, position - pair_count)
    own_inverse = lax.rsqrt(jnp.sum(pooled * pooled, axis=-1, keepdims=True) + norm_eps)
    own_unit = pooled * own_inverse
    own_low = own_unit.astype(jnp.bfloat16)
    source_rows = is_source[:, None]
    pair_match = own_pair[:, None] == pair_ids[None, :]
    toward_targets = score_scale * contract_last(own_low, targets)
    toward_sources = score_scale * contract_last(own_low, sources)
    own_scores = jnp.where(source_rows, toward_targets, toward_sources)
    own_scores = own_scores - score_scale * margin * pair_match.astype(jnp.float32)
    own_group = jnp.sum(jnp.where(pair_match, group_of[None, :], 0), axis=1)
    own_scores = jnp.where(own_group[:, None] == group_of[None, :], own_scores, masked_score)
    own_lse = jnp.sum(
        jnp.where(pair_match, jnp.where(source_rows, row_lse[None, :], col_lse[None, :]), 0.0),
        axis=1,
    )
    other_lse = jnp.where(source_rows, col_lse[None, :], row_lse[None, :])
    grad_coeff = loss_scale / pair_count
    grad_scores = grad_coeff * (
        jnp.exp(own_scores - own_lse[:, None])
        + jnp.exp(own_scores - other_lse)
        - 2.0 * pair_match.astype(jnp.float32)
    )
    grad_low = grad_scores.astype(jnp.bfloat16)
    grad_unit = score_scale * jnp.where(
        source_rows, product(grad_low, targets), product(grad_low, sources)
    )
    grad_pooled = own_inverse * (
        grad_unit - own_unit * jnp.sum(grad_unit * own_unit, axis=-1, keepdims=True)
    )
    return (loss_value, grad_pooled)


def local(
    tokens, query_weight, key_weight, value_weight, output_weight, up_weight, down_weight,
    query_bias, value_bias, output_bias, first_gain, first_shift, up_bias, down_bias,
    second_gain, second_shift, group_sizes, sentence_order,
):
    dp = lax.axis_size("dp")
    orders = rows_orders(dp)
    core = lax.axis_index("tensor").astype(jnp.int32)
    dp_index = lax.axis_index("dp").astype(jnp.int32)
    where = jnp.stack([dp_index, core])
    head_cols = query_weight.shape[1]
    hidden_cols = up_weight.shape[1]
    line = lambda vector: vector.reshape(1, -1)

    qkv_a, qkv_b = gather_rows(
        jnp.concatenate([query_weight, key_weight, value_weight], axis=1), QKV_SPLIT
    )
    up_a, up_b = gather_rows(jnp.concatenate([output_weight, up_weight], axis=1), UP_SPLIT)
    down_a, down_b = gather_rows(down_weight, hidden_cols // 2)
    parts = (
        up_a, up_b, swap_cores(up_a), swap_cores(up_b), down_a, down_b, swap_cores(down_a), swap_cores(down_b),
    )

    queries, key_rows, values, context, probs = attention_forward(
        orders, where, tokens, line(query_bias), line(value_bias), qkv_a, qkv_b
    )
    context_other = swap_cores(half_of(context, 1 - core))
    vectors = (
        line(output_bias), line(first_gain), line(first_shift), line(up_bias), line(swap_cores(up_bias)),
        line(down_bias), line(second_gain), line(second_shift),
    )
    hidden_low, normed_one, inv_one, act, slope, normed_two, inv_two, pooled, unit = feed_forward(
        orders, where, tokens, context, context_other, vectors, parts
    )
    pooled = pooled.reshape(-1, D)
    unit_low = unit.reshape(-1, D).astype(bf16)
    if dp == 16:
        units_own, units_other = gather_units(unit_low)
        loss, grad_pooled = pair_gradient(
            orders[0], where, group_sizes, sentence_order, units_own, units_other, pooled
        )
        loss_value = loss[0, 0]
    else:
        units = lax.all_gather(unit_low, ("dp", "tensor"), axis=0, tiled=True)
        loss_value, grad_pooled = pair_objective(units, pooled, group_sizes, sentence_order, dp_index * 2 + core)

    second, ffn_low, down_grad, sums_two = down_gradient(
        orders, where, grad_pooled, normed_two, inv_two, line(second_gain), act
    )
    down_other = swap_cores(down_grad[2:])
    up_grad, up_sums, residual, context_grad_own, context_grad_other, out_grad, sums_one = up_gradient(
        orders, where, second, ffn_low, slope, hidden_low, normed_one, inv_one, line(first_gain),
        context, context_other, parts,
    )
    context_grad = swap_cores(context_grad_other)
    chip_down = add_low(down_grad[:2], down_other)
    shard_down = reduce_rows(chip_down[0], chip_down[1])
    chip_up = add_low(up_grad[:2], swap_cores(up_grad[2:]))
    chip_out = add_low(out_grad[0], swap_cores(out_grad[1]))
    shard_up_out = reduce_rows(
        jnp.concatenate([chip_up[0], chip_out[:, :OUT_SPLIT]], axis=1),
        jnp.concatenate([chip_up[1], chip_out[:, OUT_SPLIT:]], axis=1),
    )
    half = hidden_cols // 2
    shard_up = jnp.concatenate(
        [shard_up_out[:, :half], shard_up_out[:, half + OUT_SPLIT : 2 * half + OUT_SPLIT]], axis=1
    )
    shard_output = jnp.concatenate(
        [shard_up_out[:, half : half + OUT_SPLIT], shard_up_out[:, 2 * half + OUT_SPLIT :]], axis=1
    )

    terms_other, my_grad, grad_a, grad_b, qkv_sums = attention_backward(
        orders, where, tokens, queries, key_rows, values, probs, context_grad, context_grad_own, residual,
        qkv_a, qkv_b,
    )
    shard_qkv = reduce_rows(grad_a, grad_b)
    shard_query = shard_qkv[:, :head_cols]
    shard_key = shard_qkv[:, head_cols : 2 * head_cols]
    shard_value = shard_qkv[:, 2 * head_cols :]
    my_grad = my_grad + swap_cores(terms_other).astype(f32)
    their_grad = swap_cores(my_grad)
    grad_tokens = jnp.concatenate(
        [jnp.where(core == 0, my_grad, their_grad), jnp.where(core == 0, their_grad, my_grad)], axis=0
    )

    sums = jnp.concatenate([sums_two[:3], sums_one[:3]], axis=0)
    sums = sums + swap_cores(sums)
    up_sums = up_sums[:, 0, :]
    up_sums = up_sums[:2] + swap_cores(up_sums[2:])
    early = sum_small(jnp.concatenate([sums, up_sums], axis=0))
    qkv_sums = sum_small(qkv_sums[0])
    return (
        loss_value, grad_tokens, shard_query, shard_key, shard_value, shard_output, shard_up, shard_down,
        qkv_sums[:head_cols], qkv_sums[2 * head_cols :], early[5], early[3], early[4], early[6:8].reshape(-1),
        early[2], early[0], early[1],
    )


def half_of(array, index):
    rows = array.shape[0] // 2
    return lax.dynamic_slice_in_dim(array, index * rows, rows, 0)


def add_low(own, other):
    return (own.astype(f32) + other.astype(f32)).astype(bf16)


QKV_SPLIT = 640
UP_SPLIT = 1024


def solution(mesh):
    placed = (
        P("dp", None),
        P("dp", "tensor"),
        P("dp", "tensor"),
        P("dp", "tensor"),
        P("dp", "tensor"),
        P("dp", "tensor"),
        P("dp", "tensor"),
        P("tensor"),
        P("tensor"),
        P(),
        P(),
        P(),
        P("tensor"),
        P(),
        P(),
        P(),
        P(),
        P(),
    )
    return jax.shard_map(
        local,
        mesh=mesh,
        in_specs=placed,
        out_specs=(
            P(),
            P("dp", None),
            P("dp", "tensor"),
            P("dp", "tensor"),
            P("dp", "tensor"),
            P("dp", "tensor"),
            P("dp", "tensor"),
            P("dp", "tensor"),
            P("tensor"),
            P("tensor"),
            P(),
            P(),
            P(),
            P("tensor"),
            P(),
            P(),
            P(),
        ),
        check_vma=False,
    )
```
